32 devices in a mesh: sample: 2 (over y), wire: 4 (over z), xsec: 2 (over x), cols: 2 (over core).
Axes of the slice: x: 2, y: 2, z: 4, core: 2. Of those that a mesh axis runs over, the one named last changes fastest.
Arguments:
- blocks: bfloat16 [32, 2, 64, 1728], P(('sample', 'wire'), 'xsec'), parts along dimension 0, may hold values from -0.109375 to 0.109375
- pattern: int32 [32, 2, 27], P(('sample', 'wire'), 'xsec'), parts along dimension 0, may hold values 0 or 1
- current: bfloat16 [32, 2, 64, 2, 512], P(('sample', 'wire'), 'xsec', None, None, 'cols'), parts along dimension 0, may hold values from -6 to 6
- previous: bfloat16 [32, 2, 64, 2, 512], P(('sample', 'wire'), 'xsec', None, None, 'cols'), parts along dimension 0, may hold values from -6 to 6
- accum: float32 [32, 2, 64, 2, 512], P(('sample', 'wire'), 'xsec', None, None, 'cols'), parts along dimension 0, may hold values from -6 to 6
- coefs: float32 [4], replicated, may hold values from 0.3 to 1
- sketch: bfloat16 [32, 2, 64, 512], P(('sample', 'wire'), 'xsec'), parts along dimension 0, may hold values from -6 to 6
- signs: int32 [32, 2, 64, 512], P(('sample', 'wire'), 'xsec', None, 'cols'), parts along dimension 0, may hold values from 0 to 1
Outputs:
- newest: bfloat16 [32, 2, 64, 2, 512], P(('sample', 'wire'), 'xsec', None, None, 'cols'), parts along dimension 0
- before: bfloat16 [32, 2, 64, 2, 512], P(('sample', 'wire'), 'xsec', None, None, 'cols'), parts along dimension 0
- summed: float32 [32, 2, 64, 2, 512], P(('sample', 'wire'), 'xsec', None, None, 'cols'), parts along dimension 0
- gram: float32 [1024, 512], P(('sample', 'wire', 'xsec'), 'cols'), parts along dimension 0
- quadratic: float32 [1024], P(('sample', 'cols')), parts along dimension 0
The draws below stay inside these ranges and needn't reach their ends.
There are 2 independent parts, one for each index of `sample`. The reference program is written for one: setup_inputs(seed, part) draws one part's arguments, and reference() takes and returns one part's arrays. A program takes and returns all parts, laid end to end along the dimension named above; an argument that names none is the same for every part. Nothing has to cross between parts.
All inputs are finite; a program needn't handle non-finite values. No bound on the sum of `pattern` on one device may be relied on, other than what follows from the above.
Results may differ from the reference program's by a relative error of at most 0.0065.
Values may be sent and summed in bfloat16 or wider, within the bound.
A program may use at most 64 MiB of HBM per device.

```python
import jax
import jax.numpy as jnp
from jax import lax

ORB = 64
REACH = 4
NCOL = 512
STEPS = 4
CELLS = 16
TILES = 2
NBLK = 27


def with_ends(array, stream_key, low, high):
    spot = [jax.random.randint(jax.random.fold_in(stream_key, axis), (), 0, length) for axis, length in enumerate(array.shape)]
    longest = array.shape.index(max(array.shape))
    next_to = spot[:longest] + [(spot[longest] + 1) % array.shape[longest]] + spot[longest + 1:]
    return array.at[tuple(spot)].set(low).at[tuple(next_to)].set(high)


def strengthened(values, stream_key, source, target, blocks, factor):
    def block_of(axis_at):
        return (jnp.arange(values.shape[axis_at]) // (values.shape[axis_at] // blocks)).reshape((-1,) + (1,) * (values.ndim - 1 - axis_at))

    one_side = jax.random.permutation(stream_key, blocks)[block_of(target)]
    second = (block_of(target) + blocks // 2) % blocks
    return jnp.where((block_of(source) == one_side) | (block_of(source) == second), factor * values, values)


def level_of(stream_key, shape, cuts, smallest, top_value):
    def one(axis_at, parts):
        heights = jax.random.uniform(jax.random.fold_in(jax.random.fold_in(stream_key, 6), axis_at), (parts,), jnp.float32, smallest / len(cuts), top_value / len(cuts))
        return jnp.repeat(jnp.exp(heights), shape[axis_at] // parts).reshape((-1,) + (1,) * (len(shape) - axis_at - 1))

    level = one(*cuts[0])
    for cut in cuts[1:]:
        level = level * one(*cut)
    return level


def gaussian(rng, shape, deviation, bound, cuts=(), kind=jnp.bfloat16):
    drawn = deviation * jax.random.normal(rng, shape, jnp.float32)
    if cuts:
        drawn = drawn * level_of(rng, shape, cuts, -0.22, 0.18)
    return jnp.clip(drawn, -bound, bound).astype(kind)


def noise_with(own_key, shape, deviation, reach, split, heavy, kind=jnp.bfloat16):
    values = deviation * jax.random.normal(own_key, shape, jnp.float32)
    if split:
        values = values * level_of(own_key, shape, split, -0.22, 0.18)
    return jnp.clip(strengthened(values, jax.random.fold_in(own_key, 3), *heavy), -reach, reach).astype(kind)


def setup_inputs(seed: int = 0, part: int = 0) -> dict:
    keys = jax.random.split(jax.random.key(seed), 9)
    own_keys = jax.random.split(jax.random.fold_in(keys[8], part), 9)
    blocks = gaussian(own_keys[0], (CELLS, TILES, ORB, NBLK * ORB), (2 * NBLK * ORB) ** -0.5, 0.109375, ((0, 4), (1, 2)))
    pattern = with_ends((jax.random.randint(own_keys[1], (CELLS, TILES, NBLK), 0, 4) < 3).astype(jnp.int32), jax.random.fold_in(own_keys[1], 1), 0, 1)
    current = gaussian(own_keys[2], (CELLS, TILES, ORB, 2, NCOL), 1.0, 6.0, ((0, 4), (1, 2), (4, 2)))
    previous = gaussian(own_keys[3], (CELLS, TILES, ORB, 2, NCOL), 1.0, 6.0, ((0, 4), (1, 2), (4, 2)))
    accum = gaussian(own_keys[4], (CELLS, TILES, ORB, 2, NCOL), 1.0, 6.0, ((0, 4), (1, 2), (4, 2)), jnp.float32)
    coefs = jnp.clip(jax.random.uniform(keys[5], (STEPS,), jnp.float32, 0.3, 1.0), 0.3, 1.0)
    sketch = noise_with(own_keys[6], (CELLS, TILES, ORB, NCOL), 1.0, 6.0, ((0, 4), (1, 2)), (0, 3, 4, 2.0))
    signs = with_ends(jax.random.randint(own_keys[7], (CELLS, TILES, ORB, NCOL), 0, 2), jax.random.fold_in(own_keys[7], 1), 0, 1).astype(jnp.int32)
    return dict(blocks=blocks, pattern=pattern, current=current, previous=previous, accum=accum, coefs=coefs, sketch=sketch, signs=signs)


def apply_operator(field, blocks, pattern):
    ext = jnp.concatenate([field[-REACH:], field, field[:REACH]], axis=0)
    ext = jnp.pad(ext, ((0, 0), (1, 1), (0, 0), (0, 0), (0, 0)))

    def one_cell(cell):
        window = lax.dynamic_slice_in_dim(ext, cell, 2 * REACH + 1, 0)
        pieces = [window[d, e:e + TILES] for d in range(2 * REACH + 1) for e in range(3)]
        stack = jnp.stack(pieces, axis=1).astype(jnp.float32)
        weights = lax.dynamic_index_in_dim(pattern, cell, 0, keepdims=False).astype(jnp.float32)
        stack = stack * weights[:, :, None, None, None]
        stack = stack.reshape(TILES, NBLK * ORB, 2 * NCOL)
        rows = lax.dynamic_index_in_dim(blocks, cell, 0, keepdims=False).astype(jnp.float32)
        out = jnp.einsum('tik,tkn->tin', rows, stack)
        return out.reshape(TILES, ORB, 2, NCOL)
    return lax.map(one_cell, jnp.arange(CELLS, dtype=jnp.int32))

def reference(blocks, pattern, current, previous, accum, coefs, sketch, signs):
    for step in range(STEPS):
        image = apply_operator(current, blocks, pattern)
        nxt = (2.0 * image - previous.astype(jnp.float32)).astype(jnp.bfloat16)
        accum = accum + coefs[step] * nxt.astype(jnp.float32)
        previous = current
        current = nxt
    scale = jnp.float32(1.0) / jnp.sqrt(jnp.float32(CELLS * TILES * ORB))
    sketched = accum[:, :, :, 0, :].astype(jnp.bfloat16).reshape(CELLS * TILES * ORB, NCOL)
    omega = sketch.reshape(CELLS * TILES * ORB, NCOL)
    gram = lax.dot_general(omega, sketched, (((0,), (0,)), ((), ())), preferred_element_type=jnp.float32) * scale
    plus_minus = (2 * signs - 1).astype(jnp.float32)
    quadratic = lax.optimization_barrier(jnp.sum(plus_minus * accum[:, :, :, 1, :], axis=(0, 1, 2))) * scale
    return (current, previous, accum, gram, quadratic)
```

```python
import functools
import math

import jax
import jax.numpy as jnp
from jax import lax
from jax.experimental import pallas as pl
from jax.experimental.pallas import tpu as pltpu
from jax.sharding import PartitionSpec as P

REACH = 4
STEPS = 4
MESH = pl.DeviceIdType.MESH
F32 = jnp.float32
BF16 = jnp.bfloat16


def dot(a, b):
    return jnp.dot(a, b, preferred_element_type=F32)


def kernel(n_w, n_x, scale, blocks, pattern, cur, prev, acc_in, coefs, sketch, signs,
           newest, before, summed, gram, quad,
           h_own, h_out, h_in, field, halo, part_out, part_in, image,
           g_all, g_out, g_in, q_out, q_in,
           z_send, z_recv, x_send, x_recv, h_send, h_recv, g_send, g_recv, q_send, q_recv):
    cells, orbs, _ = blocks.shape
    streams = cur.shape[0]
    w, x = lax.axis_index("wire"), lax.axis_index("xsec")
    n_off = h_out.shape[0]
    others = [(a, b) for a in range(n_w) for b in range(n_x) if a or b]

    def other(a, b):
        return lax.rem(w + a, n_w), lax.rem(x + b, n_x)

    barrier = pltpu.get_barrier_semaphore()
    for a, b in others:
        ow, ox = other(a, b)
        pl.semaphore_signal(barrier, inc=1, device_id={"wire": ow, "xsec": ox}, device_id_type=MESH)
    pl.semaphore_wait(barrier, len(others))

    pending = []

    def send(src, dst, ssem, rsem, where):
        copy = pltpu.make_async_remote_copy(
            src_ref=src, dst_ref=dst, send_sem=ssem, recv_sem=rsem,
            device_id=where, device_id_type=MESH)
        copy.start()
        pending.append(copy)
        return copy

    right, left = lax.rem(w + 1, n_w), lax.rem(w + n_w - 1, n_w)

    def send_wire(s, k):
        src = cur.at[s] if k == 0 else field.at[k - 1, s]
        return [
            send(src, halo.at[k, s, 0], z_send.at[k, s, 0], z_recv.at[k, s, 0], {"wire": right}),
            send(src, halo.at[k, s, 1], z_send.at[k, s, 1], z_recv.at[k, s, 1], {"wire": left}),
        ]

    wires = {s: send_wire(s, 0) for s in range(streams)}

    if n_x == 1:
        weights = []
    elif n_x == 2:
        low = (x == 1).astype(F32)
        weights = [{0: low, 2: 1.0 - low}]
        to = [1 - x]
        back = [1 - x]
    else:
        weights = [{2: (x < n_x - 1).astype(F32)}, {0: (x > 0).astype(F32)}]
        to = [lax.rem(x + 1, n_x), lax.rem(x + n_x - 1, n_x)]
        back = [to[1], to[0]]

    def banded(c, part, weight):
        pieces = []
        for j in range(cells):
            d = part * cells + j - c
            if 0 <= d <= 2 * REACH:
                piece = None
                for e, factor in weight.items():
                    col = 3 * d + e
                    m = pattern[c, col].astype(F32)
                    if factor is not None:
                        m = m * factor
                    term = blocks[c, :, col * orbs:(col + 1) * orbs].astype(F32) * m
                    piece = term if piece is None else piece + term
                pieces.append(piece.astype(BF16))
            else:
                pieces.append(jnp.zeros((orbs, orbs), BF16))
        return jnp.concatenate(pieces, axis=1)

    rows = cells * orbs
    h_copies = {}
    for part in (1, 0, 2):
        for i, weight in enumerate(weights):
            for c in range(cells):
                h_out[i, part, c * orbs:(c + 1) * orbs, :] = banded(c, part, weight)
            h_copies[i, part] = send(h_out.at[i, part], h_in.at[i, part], h_send.at[i, part],
                                     h_recv.at[i, part], {"xsec": to[i]})
    for part in range(3):
        for c in range(cells):
            h_own[part, c * orbs:(c + 1) * orbs, :] = banded(c, part, {1: None})
    summed[...] = acc_in[...]
    for i in range(n_off):
        for part in range(3):
            h_copies[i, part].wait_recv()

    def apply(h, i, s, k):
        mine = cur[s] if k == 0 else field[k - 1, s]
        total = dot(h[i + (1,)], mine)
        total = total + dot(h[i + (0,)], halo[k, s, 0])
        return total + dot(h[i + (2,)], halo[k, s, 1])

    def step(s, k):
        for copy in wires[s]:
            copy.wait_recv()
        xs = []
        for i in range(n_off):
            part_out[k, s, i] = apply(h_in, (i,), s, k).astype(BF16)
            xs.append(send(part_out.at[k, s, i], part_in.at[k, s, i], x_send.at[k, s, i],
                           x_recv.at[k, s, i], {"xsec": back[i]}))
        image[s] = apply(h_own, (), s, k)
        for copy in xs:
            copy.wait_recv()
        total = image[s]
        for i in range(n_off):
            total = total + part_in[k, s, i].astype(F32)
        old = prev[s] if k == 0 else (cur[s] if k == 1 else field[k - 2, s])
        nxt = (2.0 * total - old.astype(F32)).astype(BF16)
        field[k, s] = nxt
        if k < STEPS - 1:
            wires[s] = send_wire(s, k + 1)
        summed[s] = summed[s] + coefs[k] * nxt.astype(F32)
        if k == STEPS - 1:
            newest[s] = nxt
        if k == STEPS - 2:
            before[s] = nxt

    half = streams // 2
    wide = cur.shape[2]
    receives = []
    mine = w * n_x + x

    def gram_part():
        for s in range(half):
            sketched = summed[s].astype(BF16)
            g = lax.dot_general(sketch[...], sketched, (((0,), (0,)), ((), ())),
                                preferred_element_type=F32)
            g = g.reshape(g_all.shape[0], g_all.shape[1], wide)
            g_all[:, :, s * wide:(s + 1) * wide] = g
            g_out[:, :, s * wide:(s + 1) * wide] = g.astype(BF16)
        for n, (a, b) in enumerate(others):
            ow, ox = other(a, b)
            receives.append(send(g_out.at[ow * n_x + ox], g_in.at[n], g_send.at[n], g_recv.at[n],
                                 {"wire": ow, "xsec": ox}))

    for k in range(STEPS):
        for s in range(streams):
            step(s, k)
            if k == STEPS - 1 and s == half - 1:
                gram_part()

    for s in range(half):
        at = slice(s * wide, (s + 1) * wide)
        pm = (2 * signs[:, at] - 1).astype(F32)
        q_out[:, at] = jnp.sum(pm * summed[half + s], axis=0, keepdims=True)
    q_copies = []
    for n, (a, b) in enumerate(others):
        ow, ox = other(a, b)
        q_copies.append(send(q_out, q_in.at[n], q_send.at[n], q_recv.at[n],
                             {"wire": ow, "xsec": ox}))
    for copy in receives:
        copy.wait_recv()
    total = g_all[mine]
    for n in range(len(others)):
        total = total + g_in[n].astype(F32)
    gram[...] = total * scale
    for copy in q_copies:
        copy.wait_recv()
    total = q_out[...]
    for n in range(len(others)):
        total = total + q_in[n]
    quad[...] = total * scale
    for copy in pending:
        copy.wait_send()


def body(n_w, n_x, blocks, pattern, current, previous, accum, coefs, sketch, signs):
    cells, tiles, orbs, wide = blocks.shape
    assert tiles == 1 and cells == REACH
    halves, cols = current.shape[3:]
    rows = cells * orbs
    streams = halves

    def split(a):
        return a.reshape(rows, halves, cols).transpose(1, 0, 2)

    def join(a):
        return a.transpose(1, 0, 2).reshape(cells, tiles, orbs, halves, cols)

    n_off = min(n_x - 1, 2)
    n_dev = n_w * n_x
    g_rows = sketch.shape[3] // n_dev
    scale = 1.0 / math.sqrt(rows * n_dev)
    vmem = pl.BlockSpec(memory_space=pltpu.VMEM)
    smem = pl.BlockSpec(memory_space=pltpu.SMEM)
    dma = pltpu.SemaphoreType.DMA
    S = jax.ShapeDtypeStruct
    out = pl.pallas_call(
        functools.partial(kernel, n_w, n_x, scale),
        out_shape=(
            S((streams, rows, cols), BF16),
            S((streams, rows, cols), BF16),
            S((streams, rows, cols), F32),
            S((g_rows, cols), F32),
            S((1, cols), F32),
        ),
        in_specs=[vmem, smem, vmem, vmem, vmem, smem, vmem, vmem],
        out_specs=(vmem,) * 5,
        scratch_shapes=[
            pltpu.VMEM((3, rows, rows), BF16),
            pltpu.VMEM((n_off, 3, rows, rows), BF16),
            pltpu.VMEM((n_off, 3, rows, rows), BF16),
            pltpu.VMEM((STEPS, streams, rows, cols), BF16),
            pltpu.VMEM((STEPS, streams, 2, rows, cols), BF16),
            pltpu.VMEM((STEPS, streams, n_off, rows, cols), BF16),
            pltpu.VMEM((STEPS, streams, n_off, rows, cols), BF16),
            pltpu.VMEM((streams, rows, cols), F32),
            pltpu.VMEM((n_dev, g_rows, cols), F32),
            pltpu.VMEM((n_dev, g_rows, cols), BF16),
            pltpu.VMEM((n_dev - 1, g_rows, cols), BF16),
            pltpu.VMEM((1, cols), F32),
            pltpu.VMEM((n_dev - 1, 1, cols), F32),
            dma((STEPS, streams, 2)),
            dma((STEPS, streams, 2)),
            dma((STEPS, streams, n_off)),
            dma((STEPS, streams, n_off)),
            dma((n_off, 3)),
            dma((n_off, 3)),
            dma((n_dev - 1,)),
            dma((n_dev - 1,)),
            dma((n_dev - 1,)),
            dma((n_dev - 1,)),
        ],
        compiler_params=pltpu.CompilerParams(
            collective_id=0, has_side_effects=True, vmem_limit_bytes=40 * 1024 * 1024),
    )(
        blocks.reshape(cells, orbs, wide), pattern.reshape(cells, -1), split(current),
        split(previous), split(accum), coefs, sketch.reshape(rows, -1), signs.reshape(rows, cols))
    newest, before, summed, gram, quad = out
    return join(newest), join(before), join(summed), gram, quad.reshape(cols)


def solution(mesh):
    return jax.shard_map(
        functools.partial(body, mesh.shape["wire"], mesh.shape["xsec"]),
        mesh=mesh,
        in_specs=(
            P(("sample", "wire"), "xsec", None, None),
            P(("sample", "wire"), "xsec", None),
            P(("sample", "wire"), "xsec", None, None, "cols"),
            P(("sample", "wire"), "xsec", None, None, "cols"),
            P(("sample", "wire"), "xsec", None, None, "cols"),
            P(),
            P(("sample", "wire"), "xsec", None, None),
            P(("sample", "wire"), "xsec", None, "cols"),
        ),
        out_specs=(
            P(("sample", "wire"), "xsec", None, None, "cols"),
            P(("sample", "wire"), "xsec", None, None, "cols"),
            P(("sample", "wire"), "xsec", None, None, "cols"),
            P(("sample", "wire", "xsec"), "cols"),
            P(("sample", "cols")),
        ),
        check_vma=False,
    )
```

```python
import functools
import math

import jax
import jax.numpy as jnp
from jax import lax
from jax.experimental import pallas as pl
from jax.experimental.pallas import tpu as pltpu
from jax.sharding import PartitionSpec as P

REACH = 4
STEPS = 4
MESH = pl.DeviceIdType.MESH
F32 = jnp.float32
BF16 = jnp.bfloat16


def dot(a, b):
    return jnp.dot(a, b, preferred_element_type=F32)


def kernel(n_w, n_x, n_c, scale, blocks, pattern, cur, prev, acc_in, coefs, sketch, signs,
           newest, before, summed, gram, quad,
           h_own, h_out, h_in, field, halo, part_out, part_in, image,
           g_all, g_out, g_in, q_out, q_in,
           z_send, z_recv, x_send, x_recv, h_send, h_recv, c_send, c_recv, g_send, g_recv,
           q_send, q_recv):
    cells, orbs, _ = blocks.shape
    halves, _, cols = cur.shape
    streams, wide = field.shape[1], field.shape[3]
    half = streams // halves

    def view(ref, s):
        return ref.at[s // half, :, pl.ds(s % half * wide, wide)]

    w, x = lax.axis_index("wire"), lax.axis_index("xsec")
    n_off = h_out.shape[0]
    others = [(a, b) for a in range(n_w) for b in range(n_x) if a or b]

    def other(a, b):
        return lax.rem(w + a, n_w), lax.rem(x + b, n_x)

    barrier = pltpu.get_barrier_semaphore()
    for a, b in others:
        ow, ox = other(a, b)
        pl.semaphore_signal(barrier, inc=1, device_id={"wire": ow, "xsec": ox}, device_id_type=MESH)
    core = lax.axis_index("cols")
    for a in range(1, n_c):
        pl.semaphore_signal(barrier, inc=1, device_id={"cols": lax.rem(core + a, n_c)},
                            device_id_type=MESH)
    pl.semaphore_wait(barrier, len(others) + n_c - 1)

    pending = []

    def send(src, dst, ssem, rsem, where):
        copy = pltpu.make_async_remote_copy(
            src_ref=src, dst_ref=dst, send_sem=ssem, recv_sem=rsem,
            device_id=where, device_id_type=MESH)
        copy.start()
        pending.append(copy)
        return copy

    right, left = lax.rem(w + 1, n_w), lax.rem(w + n_w - 1, n_w)

    def send_wire(s, k):
        src = view(cur, s) if k == 0 else field.at[k - 1, s]
        return [
            send(src, halo.at[k, s, 0], z_send.at[k, s, 0], z_recv.at[k, s, 0], {"wire": right}),
            send(src, halo.at[k, s, 1], z_send.at[k, s, 1], z_recv.at[k, s, 1], {"wire": left}),
        ]

    wires = {s: send_wire(s, 0) for s in range(streams)}

    if n_x == 1:
        weights = []
    elif n_x == 2:
        low = (x == 1).astype(F32)
        weights = [{0: low, 2: 1.0 - low}]
        to = [1 - x]
        back = [1 - x]
    else:
        weights = [{2: (x < n_x - 1).astype(F32)}, {0: (x > 0).astype(F32)}]
        to = [lax.rem(x + 1, n_x), lax.rem(x + n_x - 1, n_x)]
        back = [to[1], to[0]]

    def banded(c, part, weight):
        pieces = []
        for j in range(cells):
            d = part * cells + j - c
            if 0 <= d <= 2 * REACH:
                piece = None
                for e, factor in weight.items():
                    col = 3 * d + e
                    m = pattern[c, col].astype(F32)
                    if factor is not None:
                        m = m * factor
                    term = blocks[c, :, col * orbs:(col + 1) * orbs].astype(F32) * m
                    piece = term if piece is None else piece + term
                pieces.append(piece.astype(BF16))
            else:
                pieces.append(jnp.zeros((orbs, orbs), BF16))
        return jnp.concatenate(pieces, axis=1)

    rows = cells * orbs
    share = rows // n_c
    own_share = pl.ds(pl.multiple_of(core * share, share), share)
    h_copies = []
    for part in (1, 0, 2):
        for i, weight in enumerate(weights):
            for c in range(cells):
                h_out[i, part, c * orbs:(c + 1) * orbs, :] = banded(c, part, weight)
            h_copies.append((i, part, send(
                h_out.at[i, part, own_share], h_in.at[i, part, own_share],
                h_send.at[i, part], h_recv.at[i, part], {"xsec": to[i]})))
    for part in range(3):
        for c in range(cells):
            h_own[part, c * orbs:(c + 1) * orbs, :] = banded(c, part, {1: None})
    c_copies = []
    for i, part, copy in h_copies:
        copy.wait_recv()
        for a in range(1, n_c):
            c_copies.append(send(
                h_in.at[i, part, own_share], h_in.at[i, part, own_share],
                c_send.at[i, part, a - 1], c_recv.at[i, part, a - 1],
                {"cols": lax.rem(core + a, n_c)}))
    summed[...] = acc_in[...]
    for copy in c_copies:
        copy.wait_recv()

    def apply(h, i, s, k):
        mine = view(cur, s)[...] if k == 0 else field[k - 1, s]
        total = dot(h[i + (1,)], mine)
        total = total + dot(h[i + (0,)], halo[k, s, 0])
        return total + dot(h[i + (2,)], halo[k, s, 1])

    partials = {}

    def multiply(k, s):
        for copy in wires[s]:
            copy.wait_recv()
        partials[s] = []
        for i in range(n_off):
            part_out[k, s, i] = apply(h_in, (i,), s, k).astype(BF16)
            partials[s].append(send(
                part_out.at[k, s, i], part_in.at[k, s, i], x_send.at[k, s, i],
                x_recv.at[k, s, i], {"xsec": back[i]}))
        image[s] = apply(h_own, (), s, k)

    def advance(k, s):
        for copy in partials[s]:
            copy.wait_recv()
        total = image[s]
        for i in range(n_off):
            total = total + part_in[k, s, i].astype(F32)
        old = view((prev, cur)[k], s)[...] if k < 2 else field[k - 2, s]
        nxt = (2.0 * total - old.astype(F32)).astype(BF16)
        field[k, s] = nxt
        if k < STEPS - 1:
            wires[s] = send_wire(s, k + 1)
        acc = view(summed, s)
        acc[...] = acc[...] + coefs[k] * nxt.astype(F32)
        if k == STEPS - 1:
            view(newest, s)[...] = nxt
            if s == half - 1:
                gram_part()
            if s >= half:
                quad_part(s - half)
        if k == STEPS - 2:
            view(before, s)[...] = nxt

    receives = []
    mine = w * n_x + x

    def gram_part():
        for s in range(half):
            sketched = view(summed, s)[...].astype(BF16)
            g = lax.dot_general(sketch[...], sketched, (((0,), (0,)), ((), ())),
                                preferred_element_type=F32)
            g = g.reshape(g_all.shape[0], g_all.shape[1], wide)
            g_all[:, :, s * wide:(s + 1) * wide] = g
            g_out[:, :, s * wide:(s + 1) * wide] = g.astype(BF16)
        for n, (a, b) in enumerate(others):
            ow, ox = other(a, b)
            receives.append(send(g_out.at[ow * n_x + ox], g_in.at[n], g_send.at[n], g_recv.at[n],
                                 {"wire": ow, "xsec": ox}))

    def quad_part(s):
        at = slice(s * wide, (s + 1) * wide)
        pm = (2 * signs[:, at] - 1).astype(F32)
        q_out[:, at] = jnp.sum(pm * view(summed, half + s)[...], axis=0, keepdims=True)

    last = None
    for k in range(STEPS):
        for s in range(streams):
            multiply(k, s)
            if last is not None:
                advance(*last)
            last = (k, s)
    advance(*last)

    q_copies = []
    for n, (a, b) in enumerate(others):
        ow, ox = other(a, b)
        q_copies.append(send(q_out, q_in.at[n], q_send.at[n], q_recv.at[n],
                             {"wire": ow, "xsec": ox}))
    for copy in receives:
        copy.wait_recv()
    total = g_all[mine]
    for n in range(len(others)):
        total = total + g_in[n].astype(F32)
    gram[...] = total * scale
    for copy in q_copies:
        copy.wait_recv()
    total = q_out[...]
    for n in range(len(others)):
        total = total + q_in[n]
    quad[...] = total * scale
    for copy in pending:
        copy.wait_send()


def body(n_w, n_x, n_c, blocks, pattern, current, previous, accum, coefs, sketch, signs):
    cells, tiles, orbs, wide = blocks.shape
    assert tiles == 1 and cells == REACH
    halves, cols = current.shape[3:]
    rows = cells * orbs
    lanes = 128 if cols % 128 == 0 else cols
    streams = halves * (cols // lanes)

    def split(a):
        return a.reshape(rows, halves, cols).transpose(1, 0, 2)

    def join(a):
        return a.transpose(1, 0, 2).reshape(cells, tiles, orbs, halves, cols)

    n_off = min(n_x - 1, 2)
    n_dev = n_w * n_x
    g_rows = sketch.shape[3] // n_dev
    scale = 1.0 / math.sqrt(rows * n_dev)
    vmem = pl.BlockSpec(memory_space=pltpu.VMEM)
    smem = pl.BlockSpec(memory_space=pltpu.SMEM)
    dma = pltpu.SemaphoreType.DMA
    S = jax.ShapeDtypeStruct
    out = pl.pallas_call(
        functools.partial(kernel, n_w, n_x, n_c, scale),
        out_shape=(
            S((halves, rows, cols), BF16),
            S((halves, rows, cols), BF16),
            S((halves, rows, cols), F32),
            S((g_rows, cols), F32),
            S((1, cols), F32),
        ),
        in_specs=[vmem, smem, vmem, vmem, vmem, smem, vmem, vmem],
        out_specs=(vmem,) * 5,
        scratch_shapes=[
            pltpu.VMEM((3, rows, rows), BF16),
            pltpu.VMEM((n_off, 3, rows, rows), BF16),
            pltpu.VMEM((n_off, 3, rows, rows), BF16),
            pltpu.VMEM((STEPS, streams, rows, lanes), BF16),
            pltpu.VMEM((STEPS, streams, 2, rows, lanes), BF16),
            pltpu.VMEM((STEPS, streams, n_off, rows, lanes), BF16),
            pltpu.VMEM((STEPS, streams, n_off, rows, lanes), BF16),
            pltpu.VMEM((streams, rows, lanes), F32),
            pltpu.VMEM((n_dev, g_rows, cols), F32),
            pltpu.VMEM((n_dev, g_rows, cols), BF16),
            pltpu.VMEM((n_dev - 1, g_rows, cols), BF16),
            pltpu.VMEM((1, cols), F32),
            pltpu.VMEM((n_dev - 1, 1, cols), F32),
            dma((STEPS, streams, 2)),
            dma((STEPS, streams, 2)),
            dma((STEPS, streams, n_off)),
            dma((STEPS, streams, n_off)),
            dma((n_off, 3)),
            dma((n_off, 3)),
            dma((n_off, 3, n_c)),
            dma((n_off, 3, n_c)),
            dma((n_dev - 1,)),
            dma((n_dev - 1,)),
            dma((n_dev - 1,)),
            dma((n_dev - 1,)),
        ],
        compiler_params=pltpu.CompilerParams(
            collective_id=0, has_side_effects=True, vmem_limit_bytes=40 * 1024 * 1024),
    )(
        blocks.reshape(cells, orbs, wide), pattern.reshape(cells, -1), split(current),
        split(previous), split(accum), coefs, sketch.reshape(rows, -1), signs.reshape(rows, cols))
    newest, before, summed, gram, quad = out
    return join(newest), join(before), join(summed), gram, quad.reshape(cols)


def solution(mesh):
    return jax.shard_map(
        functools.partial(body, mesh.shape["wire"], mesh.shape["xsec"], mesh.shape["cols"]),
        mesh=mesh,
        in_specs=(
            P(("sample", "wire"), "xsec", None, None),
            P(("sample", "wire"), "xsec", None),
            P(("sample", "wire"), "xsec", None, None, "cols"),
            P(("sample", "wire"), "xsec", None, None, "cols"),
            P(("sample", "wire"), "xsec", None, None, "cols"),
            P(),
            P(("sample", "wire"), "xsec", None, None),
            P(("sample", "wire"), "xsec", None, "cols"),
        ),
        out_specs=(
            P(("sample", "wire"), "xsec", None, None, "cols"),
            P(("sample", "wire"), "xsec", None, None, "cols"),
            P(("sample", "wire"), "xsec", None, None, "cols"),
            P(("sample", "wire", "xsec"), "cols"),
            P(("sample", "cols")),
        ),
        check_vma=False,
    )
```

```python
import functools
import math

import jax
import jax.numpy as jnp
from jax import lax
from jax.experimental import pallas as pl
from jax.experimental.pallas import tpu as pltpu
from jax.sharding import PartitionSpec as P

REACH = 4
STEPS = 4
MESH = pl.DeviceIdType.MESH
F32 = jnp.float32
BF16 = jnp.bfloat16


def dot(a, b):
    return jnp.dot(a, b, preferred_element_type=F32)


def kernel(n_w, n_x, n_c, scale, blocks, pattern, cur, prev, acc_in, coefs, sketch_hbm, signs_hbm,
           newest, before, summed, gram, quad,
           h_own, h_out, h_in, field, halo, part_out, part_in, image,
           g_all, g_out, g_in, q_out, q_in,
           z_send, z_recv, x_send, x_recv, h_send, h_recv, c_send, c_recv, g_send, g_recv,
           q_send, q_recv, sketch, signs, load):
    cells, orbs, _ = blocks.shape
    halves, _, cols = cur.shape
    streams, wide = field.shape[1], field.shape[3]
    half = streams // halves

    def view(ref, s):
        return ref.at[s // half, :, pl.ds(s % half * wide, wide)]

    w, x = lax.axis_index("wire"), lax.axis_index("xsec")
    n_off = h_out.shape[0]
    others = [(a, b) for a in range(n_w) for b in range(n_x) if a or b]

    def other(a, b):
        return lax.rem(w + a, n_w), lax.rem(x + b, n_x)

    barrier = pltpu.get_barrier_semaphore()
    for a, b in others:
        ow, ox = other(a, b)
        pl.semaphore_signal(barrier, inc=1, device_id={"wire": ow, "xsec": ox}, device_id_type=MESH)
    core = lax.axis_index("cols")
    for a in range(1, n_c):
        pl.semaphore_signal(barrier, inc=1, device_id={"cols": lax.rem(core + a, n_c)},
                            device_id_type=MESH)
    pl.semaphore_wait(barrier, len(others) + n_c - 1)

    loads = [pltpu.make_async_copy(sketch_hbm, sketch, load.at[0]),
             pltpu.make_async_copy(signs_hbm, signs, load.at[1])]
    pending = []

    def send(src, dst, ssem, rsem, where):
        copy = pltpu.make_async_remote_copy(
            src_ref=src, dst_ref=dst, send_sem=ssem, recv_sem=rsem,
            device_id=where, device_id_type=MESH)
        copy.start()
        pending.append(copy)
        return copy

    right, left = lax.rem(w + 1, n_w), lax.rem(w + n_w - 1, n_w)

    def send_wire(s, k):
        src = view(cur, s) if k == 0 else field.at[k - 1, s]
        return [
            send(src, halo.at[k, s, 0], z_send.at[k, s, 0], z_recv.at[k, s, 0], {"wire": right}),
            send(src, halo.at[k, s, 1], z_send.at[k, s, 1], z_recv.at[k, s, 1], {"wire": left}),
        ]

    wires = {s: send_wire(s, 0) for s in range(streams)}

    for copy in loads:
        copy.start()

    if n_x == 1:
        weights = []
    elif n_x == 2:
        low = (x == 1).astype(F32)
        weights = [{0: low, 2: 1.0 - low}]
        to = [1 - x]
        back = [1 - x]
    else:
        weights = [{2: (x < n_x - 1).astype(F32)}, {0: (x > 0).astype(F32)}]
        to = [lax.rem(x + 1, n_x), lax.rem(x + n_x - 1, n_x)]
        back = [to[1], to[0]]

    def banded(c, part, weight):
        pieces = []
        for j in range(cells):
            d = part * cells + j - c
            if 0 <= d <= 2 * REACH:
                piece = None
                for e, factor in weight.items():
                    col = 3 * d + e
                    m = pattern[c, col].astype(F32)
                    if factor is not None:
                        m = m * factor
                    term = blocks[c, :, col * orbs:(col + 1) * orbs].astype(F32) * m
                    piece = term if piece is None else piece + term
                pieces.append(piece.astype(BF16))
            else:
                pieces.append(jnp.zeros((orbs, orbs), BF16))
        return jnp.concatenate(pieces, axis=1)

    rows = cells * orbs
    share = rows // n_c
    own_share = pl.ds(pl.multiple_of(core * share, share), share)
    h_copies = []
    for part in (1, 0, 2):
        for i, weight in enumerate(weights):
            for c in range(cells):
                h_out[i, part, c * orbs:(c + 1) * orbs, :] = banded(c, part, weight)
            h_copies.append((i, part, send(
                h_out.at[i, part, own_share], h_in.at[i, part, own_share],
                h_send.at[i, part], h_recv.at[i, part], {"xsec": to[i]})))
    for part in range(3):
        for c in range(cells):
            h_own[part, c * orbs:(c + 1) * orbs, :] = banded(c, part, {1: None})
    c_copies = []
    for i, part, copy in h_copies:
        copy.wait_recv()
        for a in range(1, n_c):
            c_copies.append(send(
                h_in.at[i, part, own_share], h_in.at[i, part, own_share],
                c_send.at[i, part, a - 1], c_recv.at[i, part, a - 1],
                {"cols": lax.rem(core + a, n_c)}))
    summed[...] = acc_in[...]
    for copy in loads:
        copy.wait()
    for copy in c_copies:
        copy.wait_recv()

    partials = {}

    def multiply(k, s):
        mine = view(cur, s)[...] if k == 0 else field[k - 1, s]
        image[s] = dot(h_own[1], mine)
        sums = [dot(h_in[i, 1], mine) for i in range(n_off)]
        for side, copy in enumerate(wires[s]):
            copy.wait_recv()
            sums = [total + dot(h_in[i, 2 * side], halo[k, s, side]) for i, total in enumerate(sums)]
        partials[s] = []
        for i in range(n_off):
            part_out[k, s, i] = sums[i].astype(BF16)
            partials[s].append(send(
                part_out.at[k, s, i], part_in.at[k, s, i], x_send.at[k, s, i],
                x_recv.at[k, s, i], {"xsec": back[i]}))
        image[s] = image[s] + (dot(h_own[0], halo[k, s, 0]) + dot(h_own[2], halo[k, s, 1]))

    def advance(k, s):
        for copy in partials[s]:
            copy.wait_recv()
        total = image[s]
        for i in range(n_off):
            total = total + part_in[k, s, i].astype(F32)
        old = view((prev, cur)[k], s)[...] if k < 2 else field[k - 2, s]
        nxt = (2.0 * total - old.astype(F32)).astype(BF16)
        field[k, s] = nxt
        if k < STEPS - 1:
            wires[s] = send_wire(s, k + 1)
        acc = view(summed, s)
        acc[...] = acc[...] + coefs[k] * nxt.astype(F32)
        if k == STEPS - 1:
            view(newest, s)[...] = nxt
            if s == half - 1:
                gram_part()
            if s >= half:
                quad_part(s - half)
        if k == STEPS - 2:
            view(before, s)[...] = nxt

    receives = []
    mine = w * n_x + x

    def gram_part():
        for s in range(half):
            sketched = view(summed, s)[...].astype(BF16)
            g = lax.dot_general(sketch[...], sketched, (((0,), (0,)), ((), ())),
                                preferred_element_type=F32)
            g = g.reshape(g_all.shape[0], g_all.shape[1], wide)
            g_all[:, :, s * wide:(s + 1) * wide] = g
            g_out[:, :, s * wide:(s + 1) * wide] = g.astype(BF16)
        for n, (a, b) in enumerate(others):
            ow, ox = other(a, b)
            receives.append(send(g_out.at[ow * n_x + ox], g_in.at[n], g_send.at[n], g_recv.at[n],
                                 {"wire": ow, "xsec": ox}))

    def quad_part(s):
        at = slice(s * wide, (s + 1) * wide)
        pm = (2 * signs[:, at] - 1).astype(F32)
        q_out[:, at] = jnp.sum(pm * view(summed, half + s)[...], axis=0, keepdims=True)

    last = None
    for k in range(STEPS):
        for s in range(streams):
            multiply(k, s)
            if last is not None:
                advance(*last)
            last = (k, s)
    advance(*last)

    q_copies = []
    for n, (a, b) in enumerate(others):
        ow, ox = other(a, b)
        q_copies.append(send(q_out, q_in.at[n], q_send.at[n], q_recv.at[n],
                             {"wire": ow, "xsec": ox}))
    for copy in receives:
        copy.wait_recv()
    total = g_all[mine]
    for n in range(len(others)):
        total = total + g_in[n].astype(F32)
    gram[...] = total * scale
    for copy in q_copies:
        copy.wait_recv()
    total = q_out[...]
    for n in range(len(others)):
        total = total + q_in[n]
    quad[...] = total * scale
    for copy in pending:
        copy.wait_send()


def body(n_w, n_x, n_c, blocks, pattern, current, previous, accum, coefs, sketch, signs):
    cells, tiles, orbs, wide = blocks.shape
    assert tiles == 1 and cells == REACH
    halves, cols = current.shape[3:]
    rows = cells * orbs
    lanes = 128 if cols % 128 == 0 else cols
    streams = halves * (cols // lanes)

    def split(a):
        return a.reshape(rows, halves, cols).transpose(1, 0, 2)

    def join(a):
        return a.transpose(1, 0, 2).reshape(cells, tiles, orbs, halves, cols)

    n_off = min(n_x - 1, 2)
    n_dev = n_w * n_x
    g_rows = sketch.shape[3] // n_dev
    scale = 1.0 / math.sqrt(rows * n_dev)
    vmem = pl.BlockSpec(memory_space=pltpu.VMEM)
    hbm = pl.BlockSpec(memory_space=pltpu.HBM)
    smem = pl.BlockSpec(memory_space=pltpu.SMEM)
    dma = pltpu.SemaphoreType.DMA
    S = jax.ShapeDtypeStruct
    out = pl.pallas_call(
        functools.partial(kernel, n_w, n_x, n_c, scale),
        out_shape=(
            S((halves, rows, cols), BF16),
            S((halves, rows, cols), BF16),
            S((halves, rows, cols), F32),
            S((g_rows, cols), F32),
            S((1, cols), F32),
        ),
        in_specs=[vmem, smem, vmem, vmem, vmem, smem, hbm, hbm],
        out_specs=(vmem,) * 5,
        scratch_shapes=[
            pltpu.VMEM((3, rows, rows), BF16),
            pltpu.VMEM((n_off, 3, rows, rows), BF16),
            pltpu.VMEM((n_off, 3, rows, rows), BF16),
            pltpu.VMEM((STEPS, streams, rows, lanes), BF16),
            pltpu.VMEM((STEPS, streams, 2, rows, lanes), BF16),
            pltpu.VMEM((STEPS, streams, n_off, rows, lanes), BF16),
            pltpu.VMEM((STEPS, streams, n_off, rows, lanes), BF16),
            pltpu.VMEM((streams, rows, lanes), F32),
            pltpu.VMEM((n_dev, g_rows, cols), F32),
            pltpu.VMEM((n_dev, g_rows, cols), BF16),
            pltpu.VMEM((n_dev - 1, g_rows, cols), BF16),
            pltpu.VMEM((1, cols), F32),
            pltpu.VMEM((n_dev - 1, 1, cols), F32),
            dma((STEPS, streams, 2)),
            dma((STEPS, streams, 2)),
            dma((STEPS, streams, n_off)),
            dma((STEPS, streams, n_off)),
            dma((n_off, 3)),
            dma((n_off, 3)),
            dma((n_off, 3, n_c)),
            dma((n_off, 3, n_c)),
            dma((n_dev - 1,)),
            dma((n_dev - 1,)),
            dma((n_dev - 1,)),
            dma((n_dev - 1,)),
            pltpu.VMEM((rows, sketch.shape[3]), BF16),
            pltpu.VMEM((rows, cols), jnp.int32),
            dma((2,)),
        ],
        compiler_params=pltpu.CompilerParams(
            collective_id=0, has_side_effects=True, vmem_limit_bytes=40 * 1024 * 1024),
    )(
        blocks.reshape(cells, orbs, wide), pattern.reshape(cells, -1), split(current),
        split(previous), split(accum), coefs, sketch.reshape(rows, -1), signs.reshape(rows, cols))
    newest, before, summed, gram, quad = out
    return join(newest), join(before), join(summed), gram, quad.reshape(cols)


def solution(mesh):
    return jax.shard_map(
        functools.partial(body, mesh.shape["wire"], mesh.shape["xsec"], mesh.shape["cols"]),
        mesh=mesh,
        in_specs=(
            P(("sample", "wire"), "xsec", None, None),
            P(("sample", "wire"), "xsec", None),
            P(("sample", "wire"), "xsec", None, None, "cols"),
            P(("sample", "wire"), "xsec", None, None, "cols"),
            P(("sample", "wire"), "xsec", None, None, "cols"),
            P(),
            P(("sample", "wire"), "xsec", None, None),
            P(("sample", "wire"), "xsec", None, "cols"),
        ),
        out_specs=(
            P(("sample", "wire"), "xsec", None, None, "cols"),
            P(("sample", "wire"), "xsec", None, None, "cols"),
            P(("sample", "wire"), "xsec", None, None, "cols"),
            P(("sample", "wire", "xsec"), "cols"),
            P(("sample", "cols")),
        ),
        check_vma=False,
    )
```
